512 devices in a mesh: sample: 8 (over z_lo, core), slab: 64 (over z_hi, x, y).
Axes of the slice: x: 4, y: 8, z: 8 (z_hi: 2, z_lo: 4; z = z_hi * 4 + z_lo), core: 2. Of those that a mesh axis runs over, the one named last changes fastest.
Arguments:
- deviation: bfloat16 [8, 19, 256, 64, 128], P('sample', None, 'slab'), may hold values from -3 to 3
- solid: int32 [8, 256, 64, 128], P('sample', 'slab'), may hold values from 0 to 1, as said below
- region: int32 [8, 256, 64, 128], P('sample', 'slab'), may hold values from 0 to 1023
Outputs:
- populations: float32 [8, 19, 256, 64, 128], P('sample', None, 'slab')
- cdf: float32 [64, 1024, 64], P('slab', 'sample')
The draws below stay inside these ranges and needn't reach their ends.
Inputs may be any that keep to these rules, and one draw needn't show every extreme that they name: `solid`: the share of rock voxels differs from z-plane to z-plane.
All inputs are finite; a program needn't handle non-finite values.
Results may differ from the reference program's by a relative error of at most 0.0003.
Values sent between devices are 32-bit elements; how exact they have to be, the bound alone decides.
No kernel may reach another device: no remote copies, remote signals or barrier semaphores. Data moves between devices by JAX's collectives and lax.ppermute only.
A program may use at most 64 MiB of HBM per device.

```python
import jax
import jax.numpy as jnp
import numpy as np
from jax import lax

Q = 19
NX = 128
NY = 64
CZ = 4
LEVELS = 64
STEPS = 2
SAMPLES = 8
NZ = 256
BLOCKS = 1024
N_SLAB = 64


def draw_solid(key, part):
    key = jax.random.fold_in(key, 11)
    first, second = jax.random.split(key)
    cutoff = jax.random.randint(first, (SAMPLES, NZ, 1, 1), 100, 900)
    rolls = jax.random.randint(second, (SAMPLES, NZ, NY, NX), 0, 1000)
    return (rolls < cutoff).astype(jnp.int32)


def set_ends(drawn, stream_key, least, top_value):
    extent = drawn.shape
    place = [jax.random.randint(jax.random.fold_in(stream_key, axis), (), 0, extent[axis]) for axis in range(len(extent))]
    drawn = drawn.at[tuple(place)].set(least)
    longest = extent.index(max(extent))
    place[longest] = (place[longest] + 1) % extent[longest]
    return drawn.at[tuple(place)].set(top_value)


def block_levels(rng, extent, pieces, least, top_value):
    def one(dim, shards_of):
        draws = jax.random.uniform(jax.random.fold_in(jax.random.fold_in(rng, 6), dim), (shards_of,), jnp.float32, least / len(pieces), top_value / len(pieces))
        return jnp.repeat(jnp.exp(draws), extent[dim] // shards_of).reshape((-1,) + (1,) * (len(extent) - dim - 1))

    level = one(*pieces[0])
    for cut in pieces[1:]:
        level = level * one(*cut)
    return level


def normal_values(stream_key, shape, width, most, cuts=(), dtype=jnp.bfloat16):
    factor_of = block_levels(stream_key, shape, cuts, -0.22, 0.18) if cuts else 1.0
    values = jax.random.normal(stream_key, shape, jnp.float32) * width * factor_of
    return jnp.minimum(jnp.maximum(values, -most), most).astype(dtype)


def setup_inputs(seed: int = 0) -> dict:
    key_list = jax.random.split(jax.random.key(seed), 4)
    deviation = normal_values(key_list[0], (SAMPLES, Q, NZ, NY, NX), 1.0, 3.0, ((0, 8), (2, 64)))
    solid = draw_solid(jax.random.fold_in(key_list[3], 71), 0)
    region = set_ends(jax.random.randint(key_list[2], (SAMPLES, NZ, NY, NX), 0, BLOCKS), jax.random.fold_in(key_list[2], 1), 0, BLOCKS - 1).astype(jnp.int32)
    return {"deviation": deviation, "solid": solid, "region": region}


AMPLITUDE = 0.3
SPEED_TOP = 0.12
VELOCITY_TABLE = [[0, 0, 0], [1, 0, 0], [-1, 0, 0], [0, 1, 0], [0, -1, 0], [0, 0, 1], [0, 0, -1], [1, 1, 0], [-1, -1, 0], [1, -1, 0], [-1, 1, 0], [1, 0, 1], [-1, 0, -1], [1, 0, -1], [-1, 0, 1], [0, 1, 1], [0, -1, -1], [0, 1, -1], [0, -1, 1]]

def lattice_tables():
    velocity = np.array(VELOCITY_TABLE)
    square = (velocity * velocity).sum(1)
    weights = np.where(square == 0, 1.0 / 3.0, np.where(square == 1, 1.0 / 18.0, 1.0 / 36.0))
    cx, cy, cz = (velocity[:, 0], velocity[:, 1], velocity[:, 2])
    rows = [np.ones(19), 19 * square - 30, (21 * square ** 2 - 53 * square + 24) / 2, cx, (5 * square - 9) * cx, cy, (5 * square - 9) * cy, cz, (5 * square - 9) * cz, 3 * cx ** 2 - square, (3 * square - 5) * (3 * cx ** 2 - square), cy ** 2 - cz ** 2, (3 * square - 5) * (cy ** 2 - cz ** 2), cx * cy, cy * cz, cx * cz, (cy ** 2 - cz ** 2) * cx, (cz ** 2 - cx ** 2) * cy, (cx ** 2 - cy ** 2) * cz]
    moment = np.stack([row * 1.0 for row in rows])
    rates = np.array([0, 1.19, 1.4, 0, 1.2, 0, 1.2, 0, 1.2, 1.25, 1.4, 1.25, 1.4, 1.25, 1.25, 1.25, 1.98, 1.98, 1.98])
    norms = (moment * moment).sum(1)
    kernel = moment.T @ ((rates / norms)[:, None] * moment)
    opposite = [0, 2, 1, 4, 3, 6, 5, 8, 7, 10, 9, 12, 11, 14, 13, 16, 15, 18, 17]
    return (velocity.astype(np.float32), weights.astype(np.float32), kernel.astype(np.float32), opposite)

def collide(field, solid_plane):
    velocity, weights, kernel, opposite = lattice_tables()
    velocity = jnp.asarray(velocity)
    weights = jnp.asarray(weights)[:, None, None, None]
    kernel = jnp.asarray(kernel)
    density = lax.optimization_barrier(jnp.sum(field, axis=0))
    momentum = jnp.einsum('qd,qzyx->dzyx', velocity, field, precision=lax.Precision.HIGHEST)
    flow = momentum / density[None]
    along = jnp.einsum('qd,dzyx->qzyx', velocity, flow, precision=lax.Precision.HIGHEST)
    usq = lax.optimization_barrier(jnp.sum(flow * flow, axis=0))
    balance = weights * density[None] * (1.0 + 3.0 * along + 4.5 * along * along - 1.5 * usq[None])
    relaxed = field - jnp.einsum('pq,qzyx->pzyx', kernel, field - balance, precision=lax.Precision.HIGHEST)
    bounced = jnp.stack([field[q] for q in opposite])
    return jnp.where(solid_plane[None] == 1, bounced, relaxed)

def speed_ramp(field, solid_plane):
    velocity, weights, kernel, opposite = lattice_tables()
    density = lax.optimization_barrier(jnp.sum(field, axis=0))
    momentum = jnp.einsum('qd,qzyx->dzyx', jnp.asarray(velocity), field, precision=lax.Precision.HIGHEST)
    flow = momentum / density[None]
    speed = jnp.sqrt(lax.optimization_barrier(jnp.sum(flow * flow, axis=0)))
    step_width = SPEED_TOP / LEVELS
    levels = (jnp.arange(LEVELS) + 1).astype(jnp.float32) * step_width
    ramp = jnp.clip((levels[:, None, None, None] - speed[None]) / step_width + 0.5, 0.0, 1.0)
    pores = (1 - solid_plane).astype(jnp.float32)
    return (ramp * pores[None]).astype(jnp.bfloat16)

def one_sample(inputs):
    deviation, solid, region = inputs
    velocity, weights, kernel, opposite = lattice_tables()
    field = jnp.asarray(weights)[:, None, None, None] * (1.0 + AMPLITUDE * deviation.astype(jnp.float32))
    moves = VELOCITY_TABLE
    for step in range(STEPS):
        post = collide(field, solid)
        field = jnp.stack([jnp.roll(post[q], (moves[q][2], moves[q][1], moves[q][0]), axis=(0, 1, 2)) for q in range(19)])
    ramp = speed_ramp(field, solid)
    slab_index = (jnp.arange(NZ) // CZ).astype(jnp.int32)
    labels = (region + BLOCKS * slab_index[:, None, None]).astype(jnp.int32).reshape(-1)
    values = ramp.astype(jnp.float32).reshape(LEVELS, -1).T
    sums = jax.ops.segment_sum(values, labels, num_segments=N_SLAB * BLOCKS)
    return (field, sums)

def reference(deviation, solid, region):
    populations, sums = lax.map(one_sample, (deviation, solid, region))
    total = lax.optimization_barrier(jnp.sum(sums, axis=0))
    scale = CZ * NY * NX * SAMPLES / BLOCKS
    cdf = (total / scale).reshape(N_SLAB, BLOCKS, LEVELS)
    return (populations, cdf)
```

```python
import functools

import jax
import jax.numpy as jnp
from jax import lax
from jax.experimental import pallas as pl
from jax.experimental.pallas import tpu as pltpu
from jax.sharding import PartitionSpec as P

LEVELS = 64
AMPLITUDE = 0.3
SPEED_TOP = 0.12
MOVES = [
    (0, 0, 0),
    (1, 0, 0),
    (-1, 0, 0),
    (0, 1, 0),
    (0, -1, 0),
    (0, 0, 1),
    (0, 0, -1),
    (1, 1, 0),
    (-1, -1, 0),
    (1, -1, 0),
    (-1, 1, 0),
    (1, 0, 1),
    (-1, 0, -1),
    (1, 0, -1),
    (-1, 0, 1),
    (0, 1, 1),
    (0, -1, -1),
    (0, 1, -1),
    (0, -1, 1),
]
OPPOSITE = [0, 2, 1, 4, 3, 6, 5, 8, 7, 10, 9, 12, 11, 14, 13, 16, 15, 18, 17]
WEIGHTS = [1.0 / 3.0] + [1.0 / 18.0] * 6 + [1.0 / 36.0] * 12
FLAT = [q for q in range(19) if MOVES[q][2] == 0]
UP = [q for q in range(19) if MOVES[q][2] == 1]
DOWN = [q for q in range(19) if MOVES[q][2] == -1]
FLAT_RUNS = ((0, 5), (7, 4))
NX, NY, CZ = 128, 64, 4
STEP = 8
VMEM_BYTES = 48 * 1024 * 1024
BF16 = jnp.bfloat16
F32 = jnp.float32


def collide(f, rock):
    sx, sy, sz = f[1] + f[2], f[3] + f[4], f[5] + f[6]
    s7, s9, s11 = f[7] + f[8], f[9] + f[10], f[11] + f[12]
    s13, s15, s17 = f[13] + f[14], f[15] + f[16], f[17] + f[18]
    dx, dy, dz = f[1] - f[2], f[3] - f[4], f[5] - f[6]
    d7, d9, d11 = f[7] - f[8], f[9] - f[10], f[11] - f[12]
    d13, d15, d17 = f[13] - f[14], f[15] - f[16], f[17] - f[18]
    sxy, sxz, syz = s7 + s9, s11 + s13, s15 + s17
    one, two = sx + (sy + sz), sxy + (sxz + syz)
    rho = f[0] + one + two
    ax, bx = d7 + d9, d11 + d13
    ay, by = d15 + d17, d7 - d9
    az, bz = d11 - d13, d15 - d17
    jx, jy, jz = dx + (ax + bx), dy + (ay + by), dz + (az + bz)
    inv = 1.0 / rho
    ux, uy, uz = jx * inv, jy * inv, jz * inv
    xx, yy, zz = jx * ux, jy * uy, jz * uz
    square = xx + yy + zz
    e = (1.19 * 19 / 2394) * (two - f[0] - square)
    eps = (1.4 / 252) * (9.0 * f[0] - 7.0 * one - 2.0 * two + 5.5 * square)
    even0 = 12.0 * eps - 30.0 * e
    base1 = -11.0 * e - 4.0 * eps
    base2 = 8.0 * e + eps
    p1, p2, px = 3.0 * sx - one, two - 3.0 * syz, 3.0 * xx - square
    pxx = (1.25 / 36) * (p1 + p2 - px)
    pixx = (1.4 / 72) * (p2 - 2.0 * p1 + 0.5 * px)
    w1, w2, pw = sy - sz, sxy - sxz, yy - zz
    pww = (1.25 / 12) * (w1 + w2 - pw)
    piww = (1.4 / 24) * (w2 - 2.0 * w1 + 0.5 * pw)
    pxy = (1.25 / 4) * (s7 - s9 - jx * uy)
    pxz = (1.25 / 4) * (s11 - s13 - jx * uz)
    pyz = (1.25 / 4) * (s15 - s17 - jy * uz)
    ua, va = pxx - 2.0 * pixx, pxx + pixx
    ub, vb = pww - 2.0 * piww, pww + piww
    qx = 0.05 * jx - 0.15 * dx
    qy = 0.05 * jy - 0.15 * dy
    qz = 0.05 * jz - 0.15 * dz
    mx = (1.98 / 8) * (ax - bx)
    my = (1.98 / 8) * (ay - by)
    mz = (1.98 / 8) * (az - bz)
    xp, xm, yp, ym = qx + mx, qx - mx, qy + my, qy - my
    zp, zm = qz + mz, qz - mz
    rest = base1 - ua
    xy, xz, yz = base2 + va + vb, base2 + va - vb, base2 - 2.0 * va
    pairs = {
        1: (base1 + 2.0 * ua, -4.0 * qx),
        3: (rest + ub, -4.0 * qy),
        5: (rest - ub, -4.0 * qz),
        7: (xy + pxy, xp + ym),
        9: (xy - pxy, xp - ym),
        11: (xz + pxz, xm + zp),
        13: (xz - pxz, xm - zp),
        15: (yz + pyz, yp + zm),
        17: (yz - pyz, yp - zm),
    }
    post = [jnp.where(rock, f[0], f[0] - even0)] + [None] * 18
    for q, (even, odd) in pairs.items():
        post[q] = jnp.where(rock, f[q + 1], f[q] - (even + odd))
        post[q + 1] = jnp.where(rock, f[q], f[q + 1] - (even - odd))
    return post


def put(ref, where, turn, value, q):
    cx, cy, _ = MOVES[q]
    if cx:
        value = pltpu.roll(value, cx % NX, 1)
    row = STEP * turn
    last = NY // STEP - 1
    if cy == 0:
        ref[where + (pl.ds(row, STEP),)] = value
    elif cy == 1 and turn == last:
        ref[where + (pl.ds(row + 1, STEP - 1),)] = value[: STEP - 1]
        ref[where + (pl.ds(0, 1),)] = value[STEP - 1 :]
    elif cy == -1 and turn == 0:
        ref[where + (pl.ds(0, STEP - 1),)] = value[1:]
        ref[where + (pl.ds(NY - 1, 1),)] = value[:1]
    else:
        ref[where + (pl.ds(row + cy, STEP),)] = value


def collide_plane(load, solid, dest):
    for turn in range(NY // STEP):
        f = [load(q, turn) for q in range(19)]
        post = collide(f, solid(turn) == 1)
        for q in range(19):
            if dest[q] is not None:
                ref, where = dest[q]
                put(ref, where, turn, post[q], q)


def initial(ref, where):
    def load(q, turn):
        low = turn // 2 * 16
        rows = ref[where + (q, pl.ds(low, 16))].astype(F32)
        rows = rows[(turn % 2) * 8 : (turn % 2) * 8 + 8]
        return WEIGHTS[q] + (WEIGHTS[q] * AMPLITUDE) * rows

    return load


def rows_of(ref, where):
    return lambda turn: ref[where + (pl.ds(STEP * turn, STEP),)]


class Copies:
    def __init__(self, sems):
        self.sems = sems
        self.used = 0
        self.open = []

    def start(self, source, target):
        copy = pltpu.make_async_copy(source, target, self.sems.at[self.used])
        self.used += 1
        copy.start()
        self.open.append(copy)
        return copy

    def finish(self):
        for copy in self.open:
            copy.wait()


def odd_slab():
    return lax.rem(lax.axis_index("slab"), 2)


def first_edges(dev, solid, s1, s2, flat, inner, dev_v, solid_v, s_v, flat_v, inner_v, sems_in, sems_out):
    odd = odd_slab()
    into, out = Copies(sems_in), Copies(sems_out)
    copies = []
    for side, z in ((0, 0), (1, CZ - 1)):
        copies.append(
            (into.start(solid.at[0, z], solid_v.at[side]), into.start(dev.at[0, :, z], dev_v.at[side]))
        )
    for side in range(2):
        for copy in copies[side]:
            copy.wait()
        slot = odd if side == 0 else 1 - odd
        away, home = (DOWN, UP) if side == 0 else (UP, DOWN)
        dest = [None] * 19
        for j, q in enumerate(FLAT):
            dest[q] = (flat_v, (side, j))
        for j, q in enumerate(away):
            dest[q] = (s_v, (slot, j))
        for j, q in enumerate(home):
            dest[q] = (inner_v, (side, j))
        collide_plane(initial(dev_v, (side,)), rows_of(solid_v, (side,)), dest)
        out.start(flat_v.at[side], flat.at[side])
        out.start(inner_v.at[side], inner.at[side])
    out.start(s_v.at[0], s1)
    out.start(s_v.at[1], s2)
    out.finish()


def first_inside(dev, solid, inner, edge, field, dev_v, solid_v, f_v, edge_v, g_v, sems_in, sems_out):
    into, out = Copies(sems_in), Copies(sems_out)
    into.start(solid.at[0, pl.ds(1, 2)], solid_v)
    into.start(dev.at[0, :, pl.ds(1, 2)], dev_v)
    for j, q in enumerate(UP):
        into.start(inner.at[0, j], f_v.at[0, q])
    for j, q in enumerate(DOWN):
        into.start(inner.at[1, j], f_v.at[1, q])
    into.finish()
    for side in range(2):
        dest = [None] * 19
        for q in FLAT:
            dest[q] = (f_v, (side, q))
        away, home = (DOWN, UP) if side == 0 else (UP, DOWN)
        for j, q in enumerate(away):
            dest[q] = (edge_v, (side, j))
        for q in home:
            dest[q] = (f_v, (1 - side, q))

        def load(q, turn, side=side):
            low = turn // 2 * 16
            rows = dev_v[q, side, pl.ds(low, 16)].astype(F32)
            rows = rows[(turn % 2) * 8 : (turn % 2) * 8 + 8]
            return WEIGHTS[q] + (WEIGHTS[q] * AMPLITUDE) * rows

        collide_plane(load, rows_of(solid_v, (side,)), dest)
    out.start(edge_v, edge)
    for side in range(2):
        z = side + 1
        dest = [(g_v, (q, z + MOVES[q][2])) for q in range(19)]
        collide_plane(
            lambda q, turn, side=side: f_v[side, q, pl.ds(STEP * turn, STEP)],
            rows_of(solid_v, (side,)),
            dest,
        )
    for low, count in FLAT_RUNS:
        run = pl.ds(low, count)
        out.start(g_v.at[run, pl.ds(1, 2)], field.at[0, run, pl.ds(1, 2)])
    for q in DOWN:
        out.start(g_v.at[q, pl.ds(0, 2)], field.at[0, q, pl.ds(0, 2)])
    for q in UP:
        out.start(g_v.at[q, pl.ds(2, 2)], field.at[0, q, pl.ds(2, 2)])
    out.finish()


def second_edges(solid, flat, edge, r1, r2, held, s1, s2, field, solid_v, flat_v, edge_v, r_v, s_v, g_v, sems_in, sems_out):
    del held
    odd = odd_slab()
    into, out = Copies(sems_in), Copies(sems_out)
    into.start(r1, r_v.at[0])
    into.start(r2, r_v.at[1])
    for side, z in ((0, 0), (1, CZ - 1)):
        into.start(solid.at[0, z], solid_v.at[side])
    into.start(flat, flat_v)
    into.start(edge, edge_v)
    into.finish()
    for side, z in ((0, 0), (1, CZ - 1)):
        slot = odd if side == 0 else 1 - odd
        away, home = (DOWN, UP) if side == 0 else (UP, DOWN)
        source = {}
        for j, q in enumerate(FLAT):
            source[q] = (flat_v, (side, j))
        for j, q in enumerate(away):
            source[q] = (edge_v, (side, j))
        for j, q in enumerate(home):
            source[q] = (r_v, (slot, j))
        dest = [None] * 19
        for q in FLAT:
            dest[q] = (g_v, (q, side))
        for j, q in enumerate(away):
            dest[q] = (s_v, (slot, j))
        for q in home:
            dest[q] = (g_v, (q, side))

        def load(q, turn, source=source):
            ref, where = source[q]
            return ref[where + (pl.ds(STEP * turn, STEP),)]

        collide_plane(load, rows_of(solid_v, (side,)), dest)
        for low, count in FLAT_RUNS:
            run = pl.ds(low, count)
            out.start(g_v.at[run, side], field.at[0, run, z])
        for q in home:
            out.start(g_v.at[q, side], field.at[0, q, z + MOVES[q][2]])
    out.start(s_v.at[0], s1)
    out.start(s_v.at[1], s2)
    out.finish()


def sums_of(values):
    total = [None] * 4
    for q, value in values.items():
        for axis, sign in enumerate((1,) + MOVES[q]):
            if sign:
                term = value if total[axis] is None else total[axis]
                if total[axis] is None:
                    total[axis] = value if sign > 0 else -value
                else:
                    total[axis] = term + value if sign > 0 else term - value
    return total


def level_codes(rho, jx, jy, jz, solid):
    inv = 1.0 / rho
    ux, uy, uz = jx * inv, jy * inv, jz * inv
    speed = jnp.sqrt(ux * ux + uy * uy + uz * uz)
    place = jnp.clip(speed * (LEVELS / SPEED_TOP) - 1.5, -2.0, 100.0)
    first = jnp.ceil(place)
    return jnp.where(solid == 1, 300.0, first), first - place


def add_regions(first, part, region, total, rows):
    def body(turn, carry):
        left, right = [], []
        for j in range(rows):
            row = turn * rows + j

            def spread(ref, row=row):
                return jnp.broadcast_to(ref[pl.ds(row, 1), :], (16, NX))

            a, b = spread(first).astype(BF16), spread(part).astype(BF16)
            label = spread(region)
            high = (label >> 8).astype(F32).astype(BF16)
            low = (label & 255).astype(F32).astype(BF16)
            count = lax.broadcasted_iota(jnp.int32, (16, NX), 0).astype(F32).astype(BF16)
            zero, one = jnp.zeros((16, NX), BF16), jnp.ones((16, NX), BF16)
            ramps = [
                jnp.clip((count + BF16(16 * g) - a) + b, BF16(0), BF16(1)) for g in range(LEVELS // 16)
            ]
            left.append(
                jnp.concatenate([jnp.where(high == BF16(h), r, zero) for h in range(4) for r in ramps], 0)
            )
            right.append(
                jnp.concatenate([jnp.where(low == count + BF16(16 * g), one, zero) for g in range(16)], 0)
            )
        total[...] += lax.dot_general(
            jnp.concatenate(left, 1),
            jnp.concatenate(right, 1),
            (((1,), (1,)), ((), ())),
            preferred_element_type=F32,
        )
        return carry

    lax.fori_loop(0, first.shape[0] // rows, body, 0)


def inside_regions(field, solid, region, table, part, f_v, solid_v, region_v, first_v, frac_v, table_v, part_v, sems_in, sems_out):
    into, out = Copies(sems_in), Copies(sems_out)
    for q in range(19):
        into.start(field.at[0, q], f_v.at[q])
    into.start(solid.at[0, pl.ds(1, 2)], solid_v)
    into.start(region.at[0, 1], region_v.at[pl.ds(0, NY)])
    into.start(region.at[0, 2], region_v.at[pl.ds(NY, NY)])
    into.finish()
    for side, z in ((0, 0), (1, CZ - 1)):
        have = FLAT + (DOWN if side == 0 else UP)
        for turn in range(NY // STEP):
            rows = pl.ds(STEP * turn, STEP)
            for k, value in enumerate(sums_of({q: f_v[q, z, rows] for q in have})):
                part_v[side, k, rows] = value
    out.start(part_v, part)
    for side in range(2):
        for turn in range(NY // STEP):
            rows = pl.ds(STEP * turn, STEP)
            total = sums_of({q: f_v[q, side + 1, rows] for q in range(19)})
            first, frac = level_codes(*total, solid_v[side, rows])
            first_v[pl.ds(NY * side + STEP * turn, STEP)] = first
            frac_v[pl.ds(NY * side + STEP * turn, STEP)] = frac
    table_v[...] = jnp.zeros_like(table_v)
    add_regions(first_v, frac_v, region_v, table_v, 64)
    out.start(table_v, table)
    out.finish()


def edge_regions(solid, region, table, part, r1, r2, held, chunks, field, solid_v, region_v, part_v, r_v, first_v, frac_v, table_v, sems_in, sems_out):
    del held
    odd = odd_slab()
    into, out = Copies(sems_in), Copies(sems_out)
    into.start(r1, r_v.at[0])
    into.start(r2, r_v.at[1])
    into.start(part, part_v)
    into.start(table, table_v)
    for side, z in ((0, 0), (1, CZ - 1)):
        into.start(solid.at[0, z], solid_v.at[side])
        into.start(region.at[0, z], region_v.at[pl.ds(NY * side, NY)])
    into.finish()
    for side, z in ((0, 0), (1, CZ - 1)):
        slot = odd if side == 0 else 1 - odd
        home = UP if side == 0 else DOWN
        for j, q in enumerate(home):
            out.start(r_v.at[slot, j], field.at[0, q, z])
        for turn in range(NY // STEP):
            rows = pl.ds(STEP * turn, STEP)
            more = sums_of({q: r_v[slot, j, rows] for j, q in enumerate(home)})
            total = [part_v[side, k, rows] + more[k] for k in range(4)]
            first, frac = level_codes(*total, solid_v[side, rows])
            first_v[pl.ds(NY * side + STEP * turn, STEP)] = first
            frac_v[pl.ds(NY * side + STEP * turn, STEP)] = frac
    add_regions(first_v, frac_v, region_v, table_v, 64)
    for chunk in range(8):
        low, half = LEVELS * (chunk // 2), NX * (chunk % 2)
        out.start(table_v.at[pl.ds(low, LEVELS), pl.ds(half, NX)], chunks.at[chunk])
    out.finish()


def add_samples(chunks, cdf):
    cdf[0] = (jnp.sum(chunks[...], axis=0) * (1.0 / 256.0)).T


HBM = pl.BlockSpec(memory_space=pltpu.HBM)


def call(kernel, name, outs, scratch, copies, flops, data, aliases=None):
    return pl.pallas_call(
        kernel,
        out_shape=[jax.ShapeDtypeStruct(shape, F32) for shape in outs],
        in_specs=[HBM] * data,
        out_specs=[HBM] * len(outs),
        scratch_shapes=[pltpu.VMEM(shape, kind) for shape, kind in scratch]
        + [pltpu.SemaphoreType.DMA((copies[0],)), pltpu.SemaphoreType.DMA((copies[1],))],
        input_output_aliases=aliases or {},
        compiler_params=pltpu.CompilerParams(vmem_limit_bytes=VMEM_BYTES),
        cost_estimate=pl.CostEstimate(flops=flops, bytes_accessed=4000000, transcendentals=0),
        name=name,
    )


def per_device(deviation, solid, region):
    i32 = jnp.int32
    slabs = lax.axis_size("slab")
    plane = (NY, NX)
    five, nine = (5,) + plane, (9,) + plane
    whole = (1, 19, CZ) + plane
    far = [(i, (i + 1) % slabs if i % 2 else (i - 1) % slabs) for i in range(slabs)]
    near = [(i, i ^ 1) for i in range(slabs)]

    def exchange(first, second):
        return lax.ppermute(first, "slab", far), lax.ppermute(second, "slab", near)

    s1, s2, flat, inner = call(
        first_edges,
        "first_edges",
        [five, five, (2,) + nine, (2,) + five],
        [
            ((2, 19) + plane, BF16),
            ((2,) + plane, i32),
            ((2,) + five, F32),
            ((2,) + nine, F32),
            ((2,) + five, F32),
        ],
        (4, 6),
        10000000,
        2,
    )(deviation, solid)
    r1, r2 = exchange(s1, s2)
    edge, field = call(
        first_inside,
        "first_inside",
        [(2,) + five, whole],
        [
            ((19, 2) + plane, BF16),
            ((2,) + plane, i32),
            ((2, 19) + plane, F32),
            ((2,) + five, F32),
            ((19, CZ) + plane, F32),
        ],
        (12, 13),
        20000000,
        3,
    )(deviation, solid, inner)
    s1, s2, field = call(
        second_edges,
        "second_edges",
        [five, five, whole],
        [
            ((2,) + plane, i32),
            ((2,) + nine, F32),
            ((2,) + five, F32),
            ((2,) + five, F32),
            ((2,) + five, F32),
            ((19, 2) + plane, F32),
        ],
        (6, 16),
        10000000,
        6,
        {5: 2},
    )(solid, flat, edge, r1, r2, field)
    r1, r2 = exchange(s1, s2)
    rows = (2 * NY, NX)
    table, part = call(
        inside_regions,
        "inside_regions",
        [(256, 256), (2, 4) + plane],
        [
            ((19, CZ) + plane, F32),
            ((2,) + plane, i32),
            (rows, i32),
            (rows, F32),
            (rows, F32),
            ((256, 256), F32),
            ((2, 4) + plane, F32),
        ],
        (22, 2),
        2000000000,
        3,
    )(field, solid, region)
    chunks, field = call(
        edge_regions,
        "edge_regions",
        [(8, LEVELS, NX), whole],
        [
            ((2,) + plane, i32),
            (rows, i32),
            ((2, 4) + plane, F32),
            ((2,) + five, F32),
            (rows, F32),
            (rows, F32),
            ((256, 256), F32),
        ],
        (8, 18),
        2000000000,
        7,
        {6: 1},
    )(solid, region, table, part, r1, r2, field)
    chunks = lax.all_to_all(chunks, "sample", 0, 0)
    cdf = pl.pallas_call(
        add_samples,
        out_shape=jax.ShapeDtypeStruct((1, NX, LEVELS), F32),
        name="add_samples",
    )(chunks)
    return field, cdf


def solution(mesh):
    return jax.shard_map(
        per_device,
        mesh=mesh,
        in_specs=(
            P("sample", None, "slab", None, None),
            P("sample", "slab", None, None),
            P("sample", "slab", None, None),
        ),
        out_specs=(P("sample", None, "slab", None, None), P("slab", "sample", None)),
        check_vma=False,
    )
```

```python
import jax
import jax.numpy as jnp
from jax import lax
from jax.experimental import pallas as pl
from jax.experimental.pallas import tpu as pltpu
from jax.sharding import PartitionSpec as P

LEVELS = 64
AMPLITUDE = 0.3
SPEED_TOP = 0.12
MOVES = [
    (0, 0, 0),
    (1, 0, 0),
    (-1, 0, 0),
    (0, 1, 0),
    (0, -1, 0),
    (0, 0, 1),
    (0, 0, -1),
    (1, 1, 0),
    (-1, -1, 0),
    (1, -1, 0),
    (-1, 1, 0),
    (1, 0, 1),
    (-1, 0, -1),
    (1, 0, -1),
    (-1, 0, 1),
    (0, 1, 1),
    (0, -1, -1),
    (0, 1, -1),
    (0, -1, 1),
]
OPPOSITE = [0, 2, 1, 4, 3, 6, 5, 8, 7, 10, 9, 12, 11, 14, 13, 16, 15, 18, 17]
WEIGHTS = [1.0 / 3.0] + [1.0 / 18.0] * 6 + [1.0 / 36.0] * 12
FLAT = [q for q in range(19) if MOVES[q][2] == 0]
UP = [q for q in range(19) if MOVES[q][2] == 1]
DOWN = [q for q in range(19) if MOVES[q][2] == -1]
FLAT_RUNS = ((0, 5), (7, 4))
EDGES = ((0, 0), (1, 3))
AWAY, HOME = (DOWN, UP), (UP, DOWN)
NX, NY, CZ = 128, 64, 4
STEP = 8
VMEM_BYTES = 40 * 1024 * 1024
BF16 = jnp.bfloat16
F32 = jnp.float32


def collide(f, rock):
    sx, sy, sz = f[1] + f[2], f[3] + f[4], f[5] + f[6]
    s7, s9, s11 = f[7] + f[8], f[9] + f[10], f[11] + f[12]
    s13, s15, s17 = f[13] + f[14], f[15] + f[16], f[17] + f[18]
    dx, dy, dz = f[1] - f[2], f[3] - f[4], f[5] - f[6]
    d7, d9, d11 = f[7] - f[8], f[9] - f[10], f[11] - f[12]
    d13, d15, d17 = f[13] - f[14], f[15] - f[16], f[17] - f[18]
    sxy, sxz, syz = s7 + s9, s11 + s13, s15 + s17
    one, two = sx + (sy + sz), sxy + (sxz + syz)
    rho = f[0] + one + two
    ax, bx = d7 + d9, d11 + d13
    ay, by = d15 + d17, d7 - d9
    az, bz = d11 - d13, d15 - d17
    jx, jy, jz = dx + (ax + bx), dy + (ay + by), dz + (az + bz)
    inv = 1.0 / rho
    ux, uy, uz = jx * inv, jy * inv, jz * inv
    xx, yy, zz = jx * ux, jy * uy, jz * uz
    square = xx + yy + zz
    e = (1.19 * 19 / 2394) * (two - f[0] - square)
    eps = (1.4 / 252) * (9.0 * f[0] - 7.0 * one - 2.0 * two + 5.5 * square)
    even0 = 12.0 * eps - 30.0 * e
    base1 = -11.0 * e - 4.0 * eps
    base2 = 8.0 * e + eps
    p1, p2, px = 3.0 * sx - one, two - 3.0 * syz, 3.0 * xx - square
    pxx = (1.25 / 36) * (p1 + p2 - px)
    pixx = (1.4 / 72) * (p2 - 2.0 * p1 + 0.5 * px)
    w1, w2, pw = sy - sz, sxy - sxz, yy - zz
    pww = (1.25 / 12) * (w1 + w2 - pw)
    piww = (1.4 / 24) * (w2 - 2.0 * w1 + 0.5 * pw)
    pxy = (1.25 / 4) * (s7 - s9 - jx * uy)
    pxz = (1.25 / 4) * (s11 - s13 - jx * uz)
    pyz = (1.25 / 4) * (s15 - s17 - jy * uz)
    ua, va = pxx - 2.0 * pixx, pxx + pixx
    ub, vb = pww - 2.0 * piww, pww + piww
    qx = 0.05 * jx - 0.15 * dx
    qy = 0.05 * jy - 0.15 * dy
    qz = 0.05 * jz - 0.15 * dz
    mx = (1.98 / 8) * (ax - bx)
    my = (1.98 / 8) * (ay - by)
    mz = (1.98 / 8) * (az - bz)
    xp, xm, yp, ym = qx + mx, qx - mx, qy + my, qy - my
    zp, zm = qz + mz, qz - mz
    rest = base1 - ua
    xy, xz, yz = base2 + va + vb, base2 + va - vb, base2 - 2.0 * va
    pairs = {
        1: (base1 + 2.0 * ua, -4.0 * qx),
        3: (rest + ub, -4.0 * qy),
        5: (rest - ub, -4.0 * qz),
        7: (xy + pxy, xp + ym),
        9: (xy - pxy, xp - ym),
        11: (xz + pxz, xm + zp),
        13: (xz - pxz, xm - zp),
        15: (yz + pyz, yp + zm),
        17: (yz - pyz, yp - zm),
    }
    post = [jnp.where(rock, f[0], f[0] - even0)] + [None] * 18
    for q, (even, odd) in pairs.items():
        post[q] = jnp.where(rock, f[q + 1], f[q] - (even + odd))
        post[q + 1] = jnp.where(rock, f[q], f[q + 1] - (even - odd))
    return post


def put(ref, where, turn, value, q):
    cx, cy, _ = MOVES[q]
    if cx:
        value = pltpu.roll(value, cx % NX, 1)
    row = STEP * turn
    last = NY // STEP - 1
    if cy == 0:
        ref[where + (pl.ds(row, STEP),)] = value
    elif cy == 1 and turn == last:
        ref[where + (pl.ds(row + 1, STEP - 1),)] = value[: STEP - 1]
        ref[where + (pl.ds(0, 1),)] = value[STEP - 1 :]
    elif cy == -1 and turn == 0:
        ref[where + (pl.ds(0, STEP - 1),)] = value[1:]
        ref[where + (pl.ds(NY - 1, 1),)] = value[:1]
    else:
        ref[where + (pl.ds(row + cy, STEP),)] = value


def collide_plane(load, solid, dest):
    for turn in range(NY // STEP):
        f = [load(q, turn) for q in range(19)]
        post = collide(f, solid(turn) == 1)
        for q in range(19):
            if dest[q] is not None:
                ref, where = dest[q]
                put(ref, where, turn, post[q], q)


def initial(ref, where):
    def load(q, turn):
        low = turn // 2 * 16
        rows = ref[where(q) + (pl.ds(low, 16),)].astype(F32)
        rows = rows[(turn % 2) * 8 : (turn % 2) * 8 + 8]
        return WEIGHTS[q] + (WEIGHTS[q] * AMPLITUDE) * rows

    return load


def rows_of(ref, where):
    return lambda turn: ref[where + (pl.ds(STEP * turn, STEP),)]


def rows_from(source):
    def load(q, turn):
        ref, where = source[q]
        where = where + (pl.ds(STEP * turn, STEP),)
        if isinstance(ref, tuple):
            return jnp.where(ref[2] == 0, ref[0][where], ref[1][where])
        return ref[where]

    return load


class Copies:
    def __init__(self, sems):
        self.sems = sems
        self.used = 0
        self.open = []

    def start(self, source, target):
        copy = pltpu.make_async_copy(source, target, self.sems.at[self.used])
        self.used += 1
        copy.start()
        self.open.append(copy)
        return copy

    def finish(self):
        for copy in self.open:
            copy.wait()


def odd_slab():
    return lax.rem(lax.axis_index("slab"), 2)


def first_edges(dev, solid, rock, s1, s2, flat, inner, dev_v, s_v, sems):
    odd = odd_slab()
    into = Copies(sems)
    into.start(solid.at[0], rock)
    for side, z in EDGES:
        into.start(dev.at[0, :, z], dev_v.at[side])
    into.open[0].wait()
    for side, z in EDGES:
        into.open[side + 1].wait()
        slot = odd if side == 0 else 1 - odd
        dest = [None] * 19
        for j, q in enumerate(FLAT):
            dest[q] = (flat, (side, j))
        for j, q in enumerate(AWAY[side]):
            dest[q] = (s_v, (slot, j))
        for j, q in enumerate(HOME[side]):
            dest[q] = (inner, (side, j))
        collide_plane(initial(dev_v, lambda q, side=side: (side, q)), rows_of(rock, (z,)), dest)
    s1[...] = s_v[0]
    s2[...] = s_v[1]


def first_inside(dev, solid, inner, edge, sums, field, dev_v, f_v, g_v, sems_in, sems_out):
    into, out = Copies(sems_in), Copies(sems_out)
    into.start(dev.at[0, :, pl.ds(1, 2)], dev_v)
    into.finish()
    for side in range(2):
        dest = [None] * 19
        for q in FLAT:
            dest[q] = (f_v, (side, q))
        for j, q in enumerate(AWAY[side]):
            dest[q] = (edge, (side, j))
        for q in HOME[side]:
            dest[q] = (f_v, (1 - side, q))
        collide_plane(initial(dev_v, lambda q, side=side: (q, side)), rows_of(solid, (side + 1,)), dest)
    for side in range(2):
        source = {q: (f_v, (side, q)) for q in range(19)}
        for j, q in enumerate(HOME[side]):
            source[q] = (inner, (side, j))
        dest = [(g_v, (q, side + 1 + MOVES[q][2])) for q in range(19)]
        collide_plane(rows_from(source), rows_of(solid, (side + 1,)), dest)
    for low, count in FLAT_RUNS:
        run = pl.ds(low, count)
        out.start(g_v.at[run, pl.ds(1, 2)], field.at[0, run, pl.ds(1, 2)])
    for q in DOWN:
        out.start(g_v.at[q, pl.ds(0, 2)], field.at[0, q, pl.ds(0, 2)])
    for q in UP:
        out.start(g_v.at[q, pl.ds(2, 2)], field.at[0, q, pl.ds(2, 2)])
    for z, have in enumerate((DOWN, FLAT + DOWN, FLAT + UP, UP)):
        for turn in range(NY // STEP):
            rows = pl.ds(STEP * turn, STEP)
            for k, value in enumerate(sums_of({q: g_v[q, z, rows] for q in have})):
                sums[z, k, rows] = value
    out.finish()


def second_edges(solid, flat, edge, r1, r2, s1, s2, flat2, inner2, s_v):
    odd = odd_slab()
    for side, z in EDGES:
        slot = odd if side == 0 else 1 - odd
        source, dest = {}, [None] * 19
        for j, q in enumerate(FLAT):
            source[q] = (flat, (side, j))
            dest[q] = (flat2, (side, j))
        for j, q in enumerate(AWAY[side]):
            source[q] = (edge, (side, j))
            dest[q] = (s_v, (slot, j))
        for j, q in enumerate(HOME[side]):
            source[q] = ((r1, r2, slot), (j,))
            dest[q] = (inner2, (side, j))
        collide_plane(rows_from(source), rows_of(solid, (z,)), dest)
    s1[...] = s_v[0]
    s2[...] = s_v[1]


def sums_of(values):
    total = [None] * 4
    for q, value in values.items():
        for axis, sign in enumerate((1,) + MOVES[q]):
            if sign:
                term = value if total[axis] is None else total[axis]
                if total[axis] is None:
                    total[axis] = value if sign > 0 else -value
                else:
                    total[axis] = term + value if sign > 0 else term - value
    return total


def level_codes(rho, jx, jy, jz, solid):
    inv = 1.0 / rho
    ux, uy, uz = jx * inv, jy * inv, jz * inv
    speed = jnp.sqrt(ux * ux + uy * uy + uz * uz)
    place = jnp.clip(speed * (LEVELS / SPEED_TOP) - 1.5, -2.0, 100.0)
    first = jnp.ceil(place)
    return jnp.where(solid == 1, 300.0, first), first - place


def add_regions(first, part, region, planes, total, rows):
    low_plane, step = planes[0], planes[1] - planes[0]

    def body(turn, carry):
        left, right = [], []
        for j in range(rows):
            row = turn * rows + j

            def spread(row):
                return jnp.broadcast_to(row, (16, NX))

            a = spread(first[pl.ds(row, 1), :]).astype(BF16)
            b = spread(part[pl.ds(row, 1), :]).astype(BF16)
            label = spread(region[0, low_plane + step * turn, pl.ds(j, 1), :])
            high = (label >> 8).astype(F32).astype(BF16)
            low = (label & 255).astype(F32).astype(BF16)
            count = lax.broadcasted_iota(jnp.int32, (16, NX), 0).astype(F32).astype(BF16)
            zero, one = jnp.zeros((16, NX), BF16), jnp.ones((16, NX), BF16)
            ramps = [
                jnp.clip((count + BF16(16 * g) - a) + b, BF16(0), BF16(1)) for g in range(LEVELS // 16)
            ]
            left.append(
                jnp.concatenate([jnp.where(high == BF16(h), r, zero) for h in range(4) for r in ramps], 0)
            )
            right.append(
                jnp.concatenate([jnp.where(low == count + BF16(16 * g), one, zero) for g in range(16)], 0)
            )
        total[...] += lax.dot_general(
            jnp.concatenate(left, 1),
            jnp.concatenate(right, 1),
            (((1,), (1,)), ((), ())),
            preferred_element_type=F32,
        )
        return carry

    lax.fori_loop(0, first.shape[0] // rows, body, 0)


def inside_regions(solid, region, sums, flat2, inner2, held, table, part, field, first_v, frac_v, sems):
    del held
    out = Copies(sems)
    for side, z in EDGES:
        for j, (low, count) in ((0, FLAT_RUNS[0]), (FLAT_RUNS[0][1], FLAT_RUNS[1])):
            out.start(flat2.at[side, pl.ds(j, count)], field.at[0, pl.ds(low, count), z])
        for j, q in enumerate(HOME[side]):
            out.start(inner2.at[side, j], field.at[0, q, z + MOVES[q][2]])
    for side, z in EDGES:
        for turn in range(NY // STEP):
            rows = pl.ds(STEP * turn, STEP)
            more = sums_of({q: flat2[side, j, rows] for j, q in enumerate(FLAT)})
            for k in range(4):
                here = sums[z, k, rows]
                part[side, k, rows] = here if more[k] is None else here + more[k]
            more = sums_of({q: inner2[side, j, rows] for j, q in enumerate(HOME[side])})
            total = [sums[side + 1, k, rows] + more[k] for k in range(4)]
            first, frac = level_codes(*total, solid[side + 1, rows])
            first_v[pl.ds(NY * side + STEP * turn, STEP)] = first
            frac_v[pl.ds(NY * side + STEP * turn, STEP)] = frac
    table[...] = jnp.zeros_like(table)
    add_regions(first_v, frac_v, region, (1, 2), table, 64)
    out.finish()


def edge_regions(solid, region, table, part, r1, r2, held, chunks, field, first_v, frac_v, table_v, sems):
    del held
    odd = odd_slab()
    out = Copies(sems)
    for which, ref in ((0, r1), (1, r2)):

        @pl.when(odd == which)
        def _(ref=ref, sem=2 * which):
            for j, q in enumerate(UP):
                pltpu.make_async_copy(ref.at[j], field.at[0, q, 0], sems.at[j]).start()

        @pl.when(odd != which)
        def _(ref=ref):
            for j, q in enumerate(DOWN):
                pltpu.make_async_copy(ref.at[j], field.at[0, q, CZ - 1], sems.at[5 + j]).start()

    for side, z in EDGES:
        slot = odd if side == 0 else 1 - odd
        for turn in range(NY // STEP):
            rows = pl.ds(STEP * turn, STEP)
            load = rows_from({q: ((r1, r2, slot), (j,)) for j, q in enumerate(HOME[side])})
            more = sums_of({q: load(q, turn) for q in HOME[side]})
            total = [part[side, k, rows] + more[k] for k in range(4)]
            first, frac = level_codes(*total, solid[z, rows])
            first_v[pl.ds(NY * side + STEP * turn, STEP)] = first
            frac_v[pl.ds(NY * side + STEP * turn, STEP)] = frac
    table_v[...] = table[...]
    add_regions(first_v, frac_v, region, (0, CZ - 1), table_v, 64)
    for chunk in range(8):
        low, half = LEVELS * (chunk // 2), NX * (chunk % 2)
        chunks[chunk] = table_v[low : low + LEVELS, half : half + NX]
    for j in range(5):
        pltpu.make_async_copy(r1.at[j], field.at[0, UP[j], 0], sems.at[j]).wait()
        pltpu.make_async_copy(r1.at[j], field.at[0, DOWN[j], CZ - 1], sems.at[5 + j]).wait()


HBM = pl.BlockSpec(memory_space=pltpu.HBM)
VMEM = pl.BlockSpec(memory_space=pltpu.VMEM)


def call(kernel, places, outs, scratch, copies, flops, aliases=None, room=VMEM_BYTES, kinds=None):
    specs = [HBM if place == "H" else VMEM for place in places]
    data = len(places) - len(outs)
    return pl.pallas_call(
        kernel,
        out_shape=[jax.ShapeDtypeStruct(shape, kind) for shape, kind in zip(outs, kinds or [F32] * len(outs))],
        in_specs=specs[:data],
        out_specs=specs[data:],
        scratch_shapes=[pltpu.VMEM(shape, dtype) for shape, dtype in scratch]
        + [pltpu.SemaphoreType.DMA((count,)) for count in copies],
        input_output_aliases=aliases or {},
        compiler_params=pltpu.CompilerParams(vmem_limit_bytes=room),
        cost_estimate=pl.CostEstimate(flops=flops, bytes_accessed=4000000, transcendentals=0),
        name=kernel.__name__,
    )


def per_device(deviation, solid, region):
    i32 = jnp.int32
    slabs = lax.axis_size("slab")
    plane = (NY, NX)
    five, nine = (5,) + plane, (9,) + plane
    whole = (1, 19, CZ) + plane
    rows = (2 * NY, NX)
    far = [(i, (i + 1) % slabs if i % 2 else (i - 1) % slabs) for i in range(slabs)]
    near = [(i, i ^ 1) for i in range(slabs)]

    def exchange(first, second):
        return lax.ppermute(first, "slab", far), lax.ppermute(second, "slab", near)

    deviation = pltpu.with_memory_space_constraint(deviation, pltpu.HBM)
    solid = pltpu.with_memory_space_constraint(solid, pltpu.HBM)
    rock, s1, s2, flat, inner = call(
        first_edges,
        "HHVVVVV",
        [(CZ,) + plane, five, five, (2,) + nine, (2,) + five],
        [((2, 19) + plane, BF16), ((2,) + five, F32)],
        (3,),
        10000000,
        kinds=(i32, F32, F32, F32, F32),
    )(deviation, solid)
    r1, r2 = exchange(s1, s2)
    edge, sums, field = call(
        first_inside,
        "HVVVVH",
        [(2,) + five, (CZ, 4) + plane, whole],
        [((19, 2) + plane, BF16), ((2, 19) + plane, F32), ((19, CZ) + plane, F32)],
        (1, 12),
        20000000,
    )(deviation, rock, inner)
    s1, s2, flat, inner = call(
        second_edges,
        "VVVVVVVVV",
        [five, five, (2,) + nine, (2,) + five],
        [((2,) + five, F32)],
        (),
        10000000,
    )(rock, flat, edge, r1, r2)
    r1, r2 = exchange(s1, s2)
    table, part, field = call(
        inside_regions,
        "VVVVVHVVH",
        [(256, 256), (2, 4) + plane, whole],
        [(rows, F32), (rows, F32)],
        (14,),
        2000000000,
        {5: 2},
    )(rock, region, sums, flat, inner, field)
    chunks, field = call(
        edge_regions,
        "VVVVVVHVH",
        [(8, LEVELS, NX), whole],
        [(rows, F32), (rows, F32), ((256, 256), F32)],
        (10,),
        2000000000,
        {6: 1},
    )(rock, region, table, part, r1, r2, field)
    chunks = lax.all_to_all(chunks, "sample", 0, 0)
    cdf = jnp.sum(chunks, axis=0) * (1.0 / 256.0)
    return field, jnp.swapaxes(cdf, 0, 1)[None]


def solution(mesh):
    return jax.shard_map(
        per_device,
        mesh=mesh,
        in_specs=(
            P("sample", None, "slab", None, None),
            P("sample", "slab", None, None),
            P("sample", "slab", None, None),
        ),
        out_specs=(P("sample", None, "slab", None, None), P("slab", "sample", None)),
        check_vma=False,
    )
```

```python
import jax
import jax.numpy as jnp
from jax import lax
from jax.experimental import pallas as pl
from jax.experimental.pallas import tpu as pltpu
from jax.sharding import PartitionSpec as P

LEVELS = 64
AMPLITUDE = 0.3
SPEED_TOP = 0.12
MOVES = [
    (0, 0, 0),
    (1, 0, 0),
    (-1, 0, 0),
    (0, 1, 0),
    (0, -1, 0),
    (0, 0, 1),
    (0, 0, -1),
    (1, 1, 0),
    (-1, -1, 0),
    (1, -1, 0),
    (-1, 1, 0),
    (1, 0, 1),
    (-1, 0, -1),
    (1, 0, -1),
    (-1, 0, 1),
    (0, 1, 1),
    (0, -1, -1),
    (0, 1, -1),
    (0, -1, 1),
]
OPPOSITE = [0, 2, 1, 4, 3, 6, 5, 8, 7, 10, 9, 12, 11, 14, 13, 16, 15, 18, 17]
WEIGHTS = [1.0 / 3.0] + [1.0 / 18.0] * 6 + [1.0 / 36.0] * 12
FLAT = [q for q in range(19) if MOVES[q][2] == 0]
UP = [q for q in range(19) if MOVES[q][2] == 1]
DOWN = [q for q in range(19) if MOVES[q][2] == -1]
FLAT_RUNS = ((0, 5), (7, 4))
EDGES = ((0, 0), (1, 3))
AWAY, HOME = (DOWN, UP), (UP, DOWN)
NX, NY, CZ = 128, 64, 4
STEP = 8
VMEM_BYTES = 40 * 1024 * 1024
BF16 = jnp.bfloat16
F32 = jnp.float32


def collide(f, rock):
    sx, sy, sz = f[1] + f[2], f[3] + f[4], f[5] + f[6]
    s7, s9, s11 = f[7] + f[8], f[9] + f[10], f[11] + f[12]
    s13, s15, s17 = f[13] + f[14], f[15] + f[16], f[17] + f[18]
    dx, dy, dz = f[1] - f[2], f[3] - f[4], f[5] - f[6]
    d7, d9, d11 = f[7] - f[8], f[9] - f[10], f[11] - f[12]
    d13, d15, d17 = f[13] - f[14], f[15] - f[16], f[17] - f[18]
    sxy, sxz, syz = s7 + s9, s11 + s13, s15 + s17
    one, two = sx + (sy + sz), sxy + (sxz + syz)
    rho = f[0] + one + two
    ax, bx = d7 + d9, d11 + d13
    ay, by = d15 + d17, d7 - d9
    az, bz = d11 - d13, d15 - d17
    jx, jy, jz = dx + (ax + bx), dy + (ay + by), dz + (az + bz)
    inv = 1.0 / rho
    ux, uy, uz = jx * inv, jy * inv, jz * inv
    xx, yy, zz = jx * ux, jy * uy, jz * uz
    square = xx + yy + zz
    e = (1.19 * 19 / 2394) * (two - f[0] - square)
    eps = (1.4 / 252) * (9.0 * f[0] - 7.0 * one - 2.0 * two + 5.5 * square)
    even0 = 12.0 * eps - 30.0 * e
    base1 = -11.0 * e - 4.0 * eps
    base2 = 8.0 * e + eps
    p1, p2, px = 3.0 * sx - one, two - 3.0 * syz, 3.0 * xx - square
    pxx = (1.25 / 36) * (p1 + p2 - px)
    pixx = (1.4 / 72) * (p2 - 2.0 * p1 + 0.5 * px)
    w1, w2, pw = sy - sz, sxy - sxz, yy - zz
    pww = (1.25 / 12) * (w1 + w2 - pw)
    piww = (1.4 / 24) * (w2 - 2.0 * w1 + 0.5 * pw)
    pxy = (1.25 / 4) * (s7 - s9 - jx * uy)
    pxz = (1.25 / 4) * (s11 - s13 - jx * uz)
    pyz = (1.25 / 4) * (s15 - s17 - jy * uz)
    ua, va = pxx - 2.0 * pixx, pxx + pixx
    ub, vb = pww - 2.0 * piww, pww + piww
    qx = 0.05 * jx - 0.15 * dx
    qy = 0.05 * jy - 0.15 * dy
    qz = 0.05 * jz - 0.15 * dz
    mx = (1.98 / 8) * (ax - bx)
    my = (1.98 / 8) * (ay - by)
    mz = (1.98 / 8) * (az - bz)
    xp, xm, yp, ym = qx + mx, qx - mx, qy + my, qy - my
    zp, zm = qz + mz, qz - mz
    rest = base1 - ua
    xy, xz, yz = base2 + va + vb, base2 + va - vb, base2 - 2.0 * va
    pairs = {
        1: (base1 + 2.0 * ua, -4.0 * qx),
        3: (rest + ub, -4.0 * qy),
        5: (rest - ub, -4.0 * qz),
        7: (xy + pxy, xp + ym),
        9: (xy - pxy, xp - ym),
        11: (xz + pxz, xm + zp),
        13: (xz - pxz, xm - zp),
        15: (yz + pyz, yp + zm),
        17: (yz - pyz, yp - zm),
    }
    post = [jnp.where(rock, f[0], f[0] - even0)] + [None] * 18
    for q, (even, odd) in pairs.items():
        post[q] = jnp.where(rock, f[q + 1], f[q] - (even + odd))
        post[q + 1] = jnp.where(rock, f[q], f[q + 1] - (even - odd))
    return post


def put(ref, where, turn, value, q):
    cx, cy, _ = MOVES[q]
    if cx:
        value = pltpu.roll(value, cx % NX, 1)
    row = STEP * turn
    last = NY // STEP - 1
    if cy == 0:
        ref[where + (pl.ds(row, STEP),)] = value
    elif cy == 1 and turn == last:
        ref[where + (pl.ds(row + 1, STEP - 1),)] = value[: STEP - 1]
        ref[where + (pl.ds(0, 1),)] = value[STEP - 1 :]
    elif cy == -1 and turn == 0:
        ref[where + (pl.ds(0, STEP - 1),)] = value[1:]
        ref[where + (pl.ds(NY - 1, 1),)] = value[:1]
    else:
        ref[where + (pl.ds(row + cy, STEP),)] = value


def collide_plane(load, solid, dest):
    for turn in range(NY // STEP):
        f = [load(q, turn) for q in range(19)]
        post = collide(f, solid(turn) == 1)
        for q in range(19):
            if dest[q] is not None:
                ref, where = dest[q]
                put(ref, where, turn, post[q], q)


def initial(ref, where):
    def load(q, turn):
        low = turn // 2 * 16
        rows = ref[where(q) + (pl.ds(low, 16),)].astype(F32)
        rows = rows[(turn % 2) * 8 : (turn % 2) * 8 + 8]
        return WEIGHTS[q] + (WEIGHTS[q] * AMPLITUDE) * rows

    return load


def rows_of(ref, where):
    return lambda turn: ref[where + (pl.ds(STEP * turn, STEP),)]


def rows_from(source):
    def load(q, turn):
        ref, where = source[q]
        where = where + (pl.ds(STEP * turn, STEP),)
        if isinstance(ref, tuple):
            return jnp.where(ref[2] == 0, ref[0][where], ref[1][where])
        return ref[where]

    return load


class Copies:
    def __init__(self, sems):
        self.sems = sems
        self.used = 0
        self.open = []

    def start(self, source, target):
        copy = pltpu.make_async_copy(source, target, self.sems.at[self.used])
        self.used += 1
        copy.start()
        self.open.append(copy)
        return copy

    def finish(self):
        for copy in self.open:
            copy.wait()


def odd_slab():
    return lax.rem(lax.axis_index("slab"), 2)


def first_edges(dev, solid, rock, s1, s2, flat, inner, dev_v, s_v, sems):
    odd = odd_slab()
    into = Copies(sems)
    into.start(solid.at[0], rock)
    for side, z in EDGES:
        into.start(dev.at[0, :, z], dev_v.at[side])
    into.open[0].wait()
    for side, z in EDGES:
        into.open[side + 1].wait()
        slot = odd if side == 0 else 1 - odd
        dest = [None] * 19
        for j, q in enumerate(FLAT):
            dest[q] = (flat, (side, j))
        for j, q in enumerate(AWAY[side]):
            dest[q] = (s_v, (slot, j))
        for j, q in enumerate(HOME[side]):
            dest[q] = (inner, (side, j))
        collide_plane(initial(dev_v, lambda q, side=side: (side, q)), rows_of(rock, (z,)), dest)
    s1[...] = s_v[0]
    s2[...] = s_v[1]


def first_inside(dev, solid, inner, edge, sums, g_v, dev_v, f_v, sems):
    into = Copies(sems)
    into.start(dev.at[0, :, pl.ds(1, 2)], dev_v)
    into.finish()
    for side in range(2):
        dest = [None] * 19
        for q in FLAT:
            dest[q] = (f_v, (side, q))
        for j, q in enumerate(AWAY[side]):
            dest[q] = (edge, (side, j))
        for q in HOME[side]:
            dest[q] = (f_v, (1 - side, q))
        collide_plane(initial(dev_v, lambda q, side=side: (q, side)), rows_of(solid, (side + 1,)), dest)
    for side in range(2):
        source = {q: (f_v, (side, q)) for q in range(19)}
        for j, q in enumerate(HOME[side]):
            source[q] = (inner, (side, j))
        dest = [(g_v, (q, side + 1 + MOVES[q][2])) for q in range(19)]
        collide_plane(rows_from(source), rows_of(solid, (side + 1,)), dest)
    for z, have in enumerate((DOWN, FLAT + DOWN, FLAT + UP, UP)):
        for turn in range(NY // STEP):
            rows = pl.ds(STEP * turn, STEP)
            for k, value in enumerate(sums_of({q: g_v[q, z, rows] for q in have})):
                sums[z, k, rows] = value


def second_edges(solid, flat, edge, r1, r2, s1, s2, flat2, inner2, s_v):
    odd = odd_slab()
    for side, z in EDGES:
        slot = odd if side == 0 else 1 - odd
        source, dest = {}, [None] * 19
        for j, q in enumerate(FLAT):
            source[q] = (flat, (side, j))
            dest[q] = (flat2, (side, j))
        for j, q in enumerate(AWAY[side]):
            source[q] = (edge, (side, j))
            dest[q] = (s_v, (slot, j))
        for j, q in enumerate(HOME[side]):
            source[q] = ((r1, r2, slot), (j,))
            dest[q] = (inner2, (side, j))
        collide_plane(rows_from(source), rows_of(solid, (z,)), dest)
    s1[...] = s_v[0]
    s2[...] = s_v[1]


def sums_of(values):
    total = [None] * 4
    for q, value in values.items():
        for axis, sign in enumerate((1,) + MOVES[q]):
            if sign:
                term = value if total[axis] is None else total[axis]
                if total[axis] is None:
                    total[axis] = value if sign > 0 else -value
                else:
                    total[axis] = term + value if sign > 0 else term - value
    return total


def level_codes(rho, jx, jy, jz, solid):
    inv = 1.0 / rho
    ux, uy, uz = jx * inv, jy * inv, jz * inv
    speed = jnp.sqrt(ux * ux + uy * uy + uz * uz)
    place = jnp.clip(speed * (LEVELS / SPEED_TOP) - 1.5, -2.0, 100.0)
    first = jnp.ceil(place)
    return jnp.where(solid == 1, 300.0, first), first - place


def add_regions(first, part, region, planes, total, rows):
    low_plane, step = planes[0], planes[1] - planes[0]

    def body(turn, carry):
        left, right = [], []
        for j in range(rows):
            row = turn * rows + j

            def spread(row):
                return jnp.broadcast_to(row, (16, NX))

            a = spread(first[pl.ds(row, 1), :]).astype(BF16)
            b = spread(part[pl.ds(row, 1), :]).astype(BF16)
            label = spread(region[0, low_plane + step * turn, pl.ds(j, 1), :])
            high = (label >> 8).astype(F32).astype(BF16)
            low = (label & 255).astype(F32).astype(BF16)
            count = lax.broadcasted_iota(jnp.int32, (16, NX), 0).astype(F32).astype(BF16)
            zero, one = jnp.zeros((16, NX), BF16), jnp.ones((16, NX), BF16)
            ramps = [
                jnp.clip((count + BF16(16 * g) - a) + b, BF16(0), BF16(1)) for g in range(LEVELS // 16)
            ]
            left.append(
                jnp.concatenate([jnp.where(high == BF16(h), r, zero) for h in range(4) for r in ramps], 0)
            )
            right.append(
                jnp.concatenate([jnp.where(low == count + BF16(16 * g), one, zero) for g in range(16)], 0)
            )
        total[...] += lax.dot_general(
            jnp.concatenate(left, 1),
            jnp.concatenate(right, 1),
            (((1,), (1,)), ((), ())),
            preferred_element_type=F32,
        )
        return carry

    lax.fori_loop(0, first.shape[0] // rows, body, 0)


def inside_regions(solid, region, sums, flat2, inner2, g_v, table, part, field, first_v, frac_v, sems):
    out = Copies(sems)
    for low, count in FLAT_RUNS:
        run = pl.ds(low, count)
        out.start(g_v.at[run, pl.ds(1, 2)], field.at[0, run, pl.ds(1, 2)])
    for q in DOWN:
        out.start(g_v.at[q, pl.ds(0, 2)], field.at[0, q, pl.ds(0, 2)])
    for q in UP:
        out.start(g_v.at[q, pl.ds(2, 2)], field.at[0, q, pl.ds(2, 2)])
    for side, z in EDGES:
        for j, (low, count) in ((0, FLAT_RUNS[0]), (FLAT_RUNS[0][1], FLAT_RUNS[1])):
            out.start(flat2.at[side, pl.ds(j, count)], field.at[0, pl.ds(low, count), z])
        for j, q in enumerate(HOME[side]):
            out.start(inner2.at[side, j], field.at[0, q, z + MOVES[q][2]])
    for side, z in EDGES:
        for turn in range(NY // STEP):
            rows = pl.ds(STEP * turn, STEP)
            more = sums_of({q: flat2[side, j, rows] for j, q in enumerate(FLAT)})
            for k in range(4):
                here = sums[z, k, rows]
                part[side, k, rows] = here if more[k] is None else here + more[k]
            more = sums_of({q: inner2[side, j, rows] for j, q in enumerate(HOME[side])})
            total = [sums[side + 1, k, rows] + more[k] for k in range(4)]
            first, frac = level_codes(*total, solid[side + 1, rows])
            first_v[pl.ds(NY * side + STEP * turn, STEP)] = first
            frac_v[pl.ds(NY * side + STEP * turn, STEP)] = frac
    table[...] = jnp.zeros_like(table)
    add_regions(first_v, frac_v, region, (1, 2), table, 64)
    out.finish()


def edge_regions(solid, region, table, part, r1, r2, held, chunks, field, first_v, frac_v, table_v, sems):
    del held
    odd = odd_slab()
    out = Copies(sems)
    for which, ref in ((0, r1), (1, r2)):

        @pl.when(odd == which)
        def _(ref=ref, sem=2 * which):
            for j, q in enumerate(UP):
                pltpu.make_async_copy(ref.at[j], field.at[0, q, 0], sems.at[j]).start()

        @pl.when(odd != which)
        def _(ref=ref):
            for j, q in enumerate(DOWN):
                pltpu.make_async_copy(ref.at[j], field.at[0, q, CZ - 1], sems.at[5 + j]).start()

    for side, z in EDGES:
        slot = odd if side == 0 else 1 - odd
        for turn in range(NY // STEP):
            rows = pl.ds(STEP * turn, STEP)
            load = rows_from({q: ((r1, r2, slot), (j,)) for j, q in enumerate(HOME[side])})
            more = sums_of({q: load(q, turn) for q in HOME[side]})
            total = [part[side, k, rows] + more[k] for k in range(4)]
            first, frac = level_codes(*total, solid[z, rows])
            first_v[pl.ds(NY * side + STEP * turn, STEP)] = first
            frac_v[pl.ds(NY * side + STEP * turn, STEP)] = frac
    table_v[...] = table[...]
    add_regions(first_v, frac_v, region, (0, CZ - 1), table_v, 64)
    for chunk in range(8):
        low, half = LEVELS * (chunk // 2), NX * (chunk % 2)
        chunks[chunk] = table_v[low : low + LEVELS, half : half + NX]
    for j in range(5):
        pltpu.make_async_copy(r1.at[j], field.at[0, UP[j], 0], sems.at[j]).wait()
        pltpu.make_async_copy(r1.at[j], field.at[0, DOWN[j], CZ - 1], sems.at[5 + j]).wait()


HBM = pl.BlockSpec(memory_space=pltpu.HBM)
VMEM = pl.BlockSpec(memory_space=pltpu.VMEM)


def call(kernel, places, outs, scratch, copies, flops, aliases=None, room=VMEM_BYTES, kinds=None):
    specs = [HBM if place == "H" else VMEM for place in places]
    data = len(places) - len(outs)
    return pl.pallas_call(
        kernel,
        out_shape=[jax.ShapeDtypeStruct(shape, kind) for shape, kind in zip(outs, kinds or [F32] * len(outs))],
        in_specs=specs[:data],
        out_specs=specs[data:],
        scratch_shapes=[pltpu.VMEM(shape, dtype) for shape, dtype in scratch]
        + [pltpu.SemaphoreType.DMA((count,)) for count in copies],
        input_output_aliases=aliases or {},
        compiler_params=pltpu.CompilerParams(vmem_limit_bytes=room),
        cost_estimate=pl.CostEstimate(flops=flops, bytes_accessed=4000000, transcendentals=0),
        name=kernel.__name__,
    )


def per_device(deviation, solid, region):
    i32 = jnp.int32
    slabs = lax.axis_size("slab")
    plane = (NY, NX)
    five, nine = (5,) + plane, (9,) + plane
    whole = (1, 19, CZ) + plane
    rows = (2 * NY, NX)
    far = [(i, (i + 1) % slabs if i % 2 else (i - 1) % slabs) for i in range(slabs)]
    near = [(i, i ^ 1) for i in range(slabs)]

    def exchange(first, second):
        return lax.ppermute(first, "slab", far), lax.ppermute(second, "slab", near)

    deviation = pltpu.with_memory_space_constraint(deviation, pltpu.HBM)
    solid = pltpu.with_memory_space_constraint(solid, pltpu.HBM)
    rock, s1, s2, flat, inner = call(
        first_edges,
        "HHVVVVV",
        [(CZ,) + plane, five, five, (2,) + nine, (2,) + five],
        [((2, 19) + plane, BF16), ((2,) + five, F32)],
        (3,),
        10000000,
        kinds=(i32, F32, F32, F32, F32),
    )(deviation, solid)
    r1, r2 = exchange(s1, s2)
    edge, sums, moved = call(
        first_inside,
        "HVVVVV",
        [(2,) + five, (CZ, 4) + plane, (19, CZ) + plane],
        [((19, 2) + plane, BF16), ((2, 19) + plane, F32)],
        (1,),
        20000000,
    )(deviation, rock, inner)
    s1, s2, flat, inner = call(
        second_edges,
        "VVVVVVVVV",
        [five, five, (2,) + nine, (2,) + five],
        [((2,) + five, F32)],
        (),
        10000000,
    )(rock, flat, edge, r1, r2)
    r1, r2 = exchange(s1, s2)
    table, part, field = call(
        inside_regions,
        "VVVVVVVVH",
        [(256, 256), (2, 4) + plane, whole],
        [(rows, F32), (rows, F32)],
        (26,),
        2000000000,
    )(rock, region, sums, flat, inner, moved)
    chunks, field = call(
        edge_regions,
        "VVVVVVHVH",
        [(8, LEVELS, NX), whole],
        [(rows, F32), (rows, F32), ((256, 256), F32)],
        (10,),
        2000000000,
        {6: 1},
    )(rock, region, table, part, r1, r2, field)
    chunks = lax.all_to_all(chunks, "sample", 0, 0)
    cdf = jnp.sum(chunks, axis=0) * (1.0 / 256.0)
    return field, jnp.swapaxes(cdf, 0, 1)[None]


def solution(mesh):
    return jax.shard_map(
        per_device,
        mesh=mesh,
        in_specs=(
            P("sample", None, "slab", None, None),
            P("sample", "slab", None, None),
            P("sample", "slab", None, None),
        ),
        out_specs=(P("sample", None, "slab", None, None), P("slab", "sample", None)),
        check_vma=False,
    )
```
